512 devices in a mesh: pipe: 32 (over y_lo, z), tensor: 16 (over x, y_hi, core).
Axes of the slice: x: 4, y: 4 (y_hi: 2, y_lo: 2; y = y_hi * 2 + y_lo), z: 16, core: 2. Of those that a mesh axis runs over, the one named last changes fastest.
Arguments:
- activations: bfloat16 [32, 256, 4096], P('pipe', 'tensor'), may hold values from -6 to 6
- hidden_grad: bfloat16 [32, 256, 14336], P('pipe', None, 'tensor'), may hold values from -0.375 to 0.375
- residual_grad: bfloat16 [32, 256, 4096], P('pipe', 'tensor'), may hold values from -0.59765625 to 0.59765625
- weight_tiles: bfloat16 [32, 16, 64, 128, 128], P('pipe', 'tensor'), may hold values from -0.1875 to 0.1875
- tile_ids: int32 [32, 16, 64], P('pipe', 'tensor'), may hold values from 0 to 223, as said below
- tile_counts: int32 [32, 16], P('pipe', 'tensor'), may hold values from 16 to 64, as said below
Outputs:
- received: bfloat16 [32, 256, 4096], P('pipe', 'tensor')
- weight_grads: bfloat16 [32, 16, 64, 128, 128], P('pipe', 'tensor')
The draws below stay inside these ranges and needn't reach their ends.
Inputs may be any that keep to these rules, and one draw needn't show every extreme that they name: `tile_ids`: within each shard's list the entries are distinct and increasing; entries at slots from that shard's count on are not read. `tile_counts`: in every section some shard has exactly 64 tiles.
All inputs are finite; a program needn't handle non-finite values.
Results may differ from the reference program's by a relative error of at most 0.001.
Values may be sent and summed in bfloat16 or wider, within the bound.
No kernel may reach another device: no remote copies, remote signals or barrier semaphores. Data moves between devices by JAX's collectives and lax.ppermute only.
A program may use at most 64 MiB of HBM per device.

```python
import jax
import jax.numpy as jnp
from jax import lax

D = 4096
FF = 14336
BLK = 128
CAP = 64
TOKENS = 256
PIPE = 32
N_PIPE = 32
N_TENSOR = 16


def ordered_draw(key_item, positions):
    return jnp.sort(jax.random.permutation(key_item, positions)[:CAP])


def tile_layout(key):
    positions = FF // (BLK * N_TENSOR) * (D // BLK)
    count_key, busy_key, order_key = jax.random.split(key, 3)
    counts = jax.random.randint(count_key, (N_PIPE, N_TENSOR), CAP // 4, CAP + 1)
    busy_shard = jax.random.randint(busy_key, (N_PIPE, 1), 0, N_TENSOR)
    counts = jnp.where(jnp.arange(N_TENSOR)[None, :] == busy_shard, CAP, counts).astype(jnp.int32)
    key_list = jax.random.split(order_key, N_PIPE * N_TENSOR)
    chosen = jax.vmap(partial_order(positions))(key_list)
    return (counts, chosen.reshape(N_PIPE, N_TENSOR, CAP).astype(jnp.int32))


def partial_order(positions):

    def inner(key_item):
        return ordered_draw(key_item, positions)
    return inner


def draw_tile_ids(key, part):
    counts, chosen = tile_layout(key)
    return chosen


def draw_tile_counts(key, part):
    counts, chosen = tile_layout(key)
    return counts


def shard_levels(rng, shape, cuts, least, largest):
    def one(position, parts):
        draws = jax.random.uniform(jax.random.fold_in(jax.random.fold_in(rng, 6), position), (parts,), jnp.float32, least / len(cuts), largest / len(cuts))
        return jnp.repeat(jnp.exp(draws), shape[position] // parts).reshape((-1,) + (1,) * (len(shape) - position - 1))

    level = one(*cuts[0])
    for cut in cuts[1:]:
        level = level * one(*cut)
    return level


def noise(rng, dims, scale, bound, shards=(), held_as=jnp.bfloat16):
    result = scale * jax.random.normal(rng, dims, jnp.float32)
    if shards:
        result = result * shard_levels(rng, dims, shards, -0.22, 0.18)
    return jnp.clip(result, -bound, bound).astype(held_as)


def setup_inputs(seed: int = 0) -> dict:
    streams_of = jax.random.split(jax.random.key(seed), 7)
    return {
        "activations": noise(streams_of[0], (PIPE, TOKENS, D), 1.0, 6.0, ((0, 32), (1, 16))),
        "hidden_grad": noise(streams_of[1], (PIPE, TOKENS, FF), (TOKENS ** -0.5), 0.375, ((0, 32), (2, 16))),
        "residual_grad": noise(streams_of[2], (PIPE, TOKENS, D), 0.1, 0.59765625, ((0, 32), (1, 16))),
        "weight_tiles": noise(streams_of[3], (PIPE, N_TENSOR, CAP, BLK, BLK), (BLK * 8) ** -0.5, 0.1875, ((0, 32), (1, 16))),
        "tile_ids": draw_tile_ids(jax.random.fold_in(streams_of[6], 71), 0),
        "tile_counts": draw_tile_counts(jax.random.fold_in(streams_of[6], 71), 0),
    }


def reference(activations, hidden_grad, residual_grad, weight_tiles, tile_ids, tile_counts):
    blocks_d = D // BLK
    blocks_h = FF // (BLK * N_TENSOR)

    def per_section(section_inputs):
        section_acts, section_grads, section_tiles, section_names, section_counts = section_inputs
        act_blocks = section_acts.astype(jnp.float32).reshape(TOKENS, blocks_d, BLK)

        def per_shard(partial_value, inputs):
            shard_tiles, shard_names, shard_count, shard_index = inputs
            local_grad = lax.dynamic_slice_in_dim(section_grads, (shard_index * blocks_h * BLK).astype(jnp.int32), blocks_h * BLK, 1)
            local_grad = local_grad.astype(jnp.float32).reshape(TOKENS, blocks_h, BLK)
            hidden_block = shard_names // blocks_d
            model_block = shard_names % blocks_d
            usable = jnp.arange(CAP, dtype=jnp.int32) < shard_count
            grad_part = jnp.take(local_grad, hidden_block, axis=1)
            act_part = jnp.take(act_blocks, model_block, axis=1)
            backward = jnp.einsum('tsk,sjk->tsj', grad_part, shard_tiles.astype(jnp.float32))
            backward = jnp.where(usable[None, :, None], backward, jnp.zeros_like(backward))
            partial_value = partial_value.at[:, model_block].add(backward)
            fresh_grads = jnp.einsum('tsj,tsk->sjk', act_part, grad_part)
            fresh_grads = jnp.where(usable[:, None, None], fresh_grads, jnp.zeros_like(fresh_grads))
            return partial_value, fresh_grads.astype(jnp.bfloat16)

        initial = jnp.zeros((TOKENS, blocks_d, BLK), jnp.float32)
        shard_order = jnp.arange(N_TENSOR, dtype=jnp.int32)
        partial_value, fresh_grads = lax.scan(per_shard, initial, (section_tiles, section_names, section_counts, shard_order))
        return partial_value.reshape(TOKENS, D), fresh_grads

    partial_value, weight_grads = lax.map(per_section, (activations, hidden_grad, weight_tiles, tile_ids, tile_counts))
    sent_grad = (residual_grad.astype(jnp.float32) + partial_value).astype(jnp.bfloat16)
    received = jnp.concatenate([sent_grad[1:], jnp.zeros_like(sent_grad[:1])], axis=0)
    return received, weight_grads
```

```python
import functools

import jax
import jax.numpy as jnp
from jax import lax
from jax.experimental import pallas as pl
from jax.experimental.pallas import tpu as pltpu
from jax.sharding import PartitionSpec as P

BLK = 128
LEVELS = 32700.0
STEPS = 128.0
FLOOR = 2.0**-100


def branch_kernel(ids, h0, w0, h1, w1, out, acc):
    rows, width = h0.shape[0] * h0.shape[1], out.shape[-1] - BLK
    blocks = width // BLK
    slots = w0.shape[0]
    unroll = 4
    acc[...] = jnp.zeros_like(acc)
    for s, (h, w) in enumerate(((h0, w0), (h1, w1))):
        live_count = ids[s, slots]

        def some(t, _, s=s, h=h, w=w, live_count=live_count):
            found = []
            for u in range(unroll):
                j = t * unroll + u
                name = ids[s, j]
                live = j < live_count
                c = jnp.where(live, name // blocks, 0)
                b = jnp.where(live, name % blocks, blocks)
                left = h[:, :, pl.ds(pl.multiple_of(c * BLK, BLK), BLK)].reshape(rows, BLK)
                d = lax.dot_general(left, w[j], (((1,), (1,)), ((), ())), preferred_element_type=jnp.float32)
                found.append((b, d))
            for b, d in found:
                at = pl.ds(pl.multiple_of(b * BLK, BLK), BLK)
                acc[:, at] += d
            return 0

        lax.fori_loop(0, (live_count + unroll - 1) // unroll, some, 0)
    lane = lax.broadcasted_iota(jnp.int32, (rows, BLK), 1)

    def code(k, scales):
        at = pl.ds(pl.multiple_of(k * BLK, BLK), BLK)
        x = acc[:, at]
        top = jnp.maximum(jnp.max(jnp.abs(x), axis=1, keepdims=True), FLOOR)
        e = jnp.ceil(STEPS * jnp.log2(top))
        y = jnp.round(x * (LEVELS * jnp.exp2(e * (-1.0 / STEPS))))
        out[:, :, at] = y.astype(jnp.int32).astype(jnp.int16).reshape(out.shape[0], out.shape[1], BLK)
        return jnp.where(lane == k, e.astype(jnp.int32), scales)

    scales = lax.fori_loop(0, blocks, code, jnp.zeros((rows, BLK), jnp.int32))
    out[:, :, width:] = scales.astype(jnp.int16).reshape(out.shape[0], out.shape[1], BLK)


def total_kernel(parts, residual, out):
    count, rows, width = parts.shape[0], out.shape[0], out.shape[1]
    scales = [
        jnp.exp2(parts[i, :, width:].astype(jnp.int32).astype(jnp.float32) * (1.0 / STEPS)) * (1.0 / LEVELS)
        for i in range(count)
    ]
    for k in range(width // BLK):
        at = slice(k * BLK, (k + 1) * BLK)
        value = jnp.zeros((rows, BLK), jnp.float32)
        for i in range(count):
            value += parts[i, :, at].astype(jnp.int32).astype(jnp.float32) * scales[i][:, k : k + 1]
        out[:, at] = (residual[:, at].astype(jnp.float32) + value).astype(out.dtype)


def weight_kernel(ids, a0, a1, h0, h1, out):
    rows = a0.shape[0] * a0.shape[1]
    blocks = a0.shape[-1] // BLK
    slots = out.shape[0]
    unroll = 4
    live_count = ids[0, slots]

    def some(t, _):
        for u in range(unroll):
            j = t * unroll + u
            name = ids[0, j]
            live = j < live_count
            c = pl.ds(pl.multiple_of(jnp.where(live, name // blocks, 0) * BLK, BLK), BLK)
            b = pl.ds(pl.multiple_of(jnp.where(live, name % blocks, 0) * BLK, BLK), BLK)
            act = jnp.concatenate([a0[:, :, b].reshape(rows, BLK), a1[:, :, b].reshape(rows, BLK)], axis=0)
            hid = jnp.concatenate([h0[:, :, c].reshape(rows, BLK), h1[:, :, c].reshape(rows, BLK)], axis=0)
            d = lax.dot_general(act, hid, (((0,), (0,)), ((), ())), preferred_element_type=jnp.float32)
            out[j] = jnp.where(live, d, 0.0).astype(out.dtype)
        return 0

    trips = (live_count + unroll - 1) // unroll
    lax.fori_loop(0, trips, some, 0)

    def clear(j, _):
        out[j] = jnp.zeros((BLK, BLK), out.dtype)
        return 0

    lax.fori_loop(trips * unroll, slots, clear, 0)


SMEM = pl.BlockSpec(memory_space=pltpu.SMEM)
VMEM = pl.BlockSpec(memory_space=pltpu.VMEM)


def shards(activations, hidden_grad, residual_grad, weight_tiles, tile_ids, tile_counts):
    count = lax.axis_size("tensor")
    chips = count // 2
    rows, width = activations.shape[1:]
    slots = weight_tiles.shape[2]
    core = lax.axis_index("tensor") % 2
    swap = [(i, i ^ 1) for i in range(count)]
    same_core = [[2 * i + c for i in range(chips)] for c in range(2)]

    tiles = weight_tiles[0, 0]
    tiles_other = lax.ppermute(tiles, "tensor", swap)
    names = jnp.concatenate([tile_ids[0, 0], tile_counts[0], jnp.zeros((7,), jnp.int32)])
    names_other = lax.ppermute(names, "tensor", swap)
    hidden = hidden_grad[0].reshape(chips, 2, rows, -1)
    hidden_here = lax.dynamic_index_in_dim(hidden, core, 1, keepdims=False)
    hidden_there = lax.dynamic_index_in_dim(hidden, 1 - core, 1, keepdims=False)
    hidden_other = lax.ppermute(hidden_there, "tensor", swap)
    acts = lax.all_to_all(
        jnp.broadcast_to(activations, (chips, rows, width)), "tensor", 0, 0, axis_index_groups=same_core, tiled=True
    )
    acts_other = lax.ppermute(acts, "tensor", swap)
    both_names = jnp.stack([names, names_other])

    sent = pl.pallas_call(
        branch_kernel,
        out_shape=jax.ShapeDtypeStruct((chips, rows, width + BLK), jnp.int16),
        in_specs=[SMEM, VMEM, VMEM, VMEM, VMEM],
        out_specs=VMEM,
        scratch_shapes=[pltpu.VMEM((chips * rows, width + BLK), jnp.float32)],
        compiler_params=pltpu.CompilerParams(vmem_limit_bytes=40 << 20),
        cost_estimate=pl.CostEstimate(flops=4 << 30, bytes_accessed=6 << 20, transcendentals=0),
        name="branch",
    )(both_names, hidden_here, tiles, hidden_other, tiles_other)
    parts = lax.all_to_all(sent, "tensor", 0, 0, axis_index_groups=same_core, tiled=True)
    grads = pl.pallas_call(
        weight_kernel,
        out_shape=jax.ShapeDtypeStruct(tiles.shape, jnp.bfloat16),
        in_specs=[SMEM, VMEM, VMEM, VMEM, VMEM],
        out_specs=VMEM,
        compiler_params=pltpu.CompilerParams(vmem_limit_bytes=40 << 20),
        cost_estimate=pl.CostEstimate(flops=4 << 30, bytes_accessed=6 << 20, transcendentals=0),
        name="weight_grads",
    )(names[None], acts, acts_other, hidden_here, hidden_there)
    total = pl.pallas_call(
        total_kernel,
        out_shape=jax.ShapeDtypeStruct((rows, width), jnp.bfloat16),
        in_specs=[VMEM, VMEM],
        out_specs=VMEM,
        compiler_params=pltpu.CompilerParams(vmem_limit_bytes=40 << 20),
        name="total",
    )(parts, residual_grad[0])
    pipes = lax.axis_size("pipe")
    received = lax.ppermute(total, "pipe", [(i, i - 1) for i in range(1, pipes)])
    return received[None], grads[None, None]


def solution(mesh):
    return jax.shard_map(
        shards,
        mesh=mesh,
        in_specs=(
            P("pipe", "tensor", None),
            P("pipe", None, "tensor"),
            P("pipe", "tensor", None),
            P("pipe", "tensor", None, None, None),
            P("pipe", "tensor", None),
            P("pipe", "tensor"),
        ),
        out_specs=(P("pipe", "tensor", None), P("pipe", "tensor", None, None, None)),
        check_vma=False,
    )
```

```python
import jax
import jax.numpy as jnp
from jax import lax
from jax.experimental import pallas as pl
from jax.experimental.pallas import tpu as pltpu
from jax.sharding import PartitionSpec as P

BLK = 128
LEVELS = 32700.0
STEPS = 128.0
FLOOR = 2.0**-100
GROUP = 16
PIECES = 2


def spread_kernel(acts, out, held, sems):
    fetch = pltpu.make_async_copy(acts.at[0], held, sems.at[0])
    fetch.start()
    fetch.wait()
    copies = [pltpu.make_async_copy(held, out.at[i], sems.at[i]) for i in range(out.shape[0])]
    for copy in copies:
        copy.start()
    for copy in copies:
        copy.wait()


def hidden_copies(hidden, held, sems):
    core = lax.axis_index("tensor") % 2
    width = hidden.shape[-1]
    return [
        pltpu.make_async_copy(hidden.at[:, which], held.at[i, :, :, pl.ds(0, width)], sems.at[i])
        for i, which in enumerate((core, 1 - core))
    ]


def encode(read, write, write_scale, blocks, rows):
    top = jnp.full((rows, BLK), FLOOR, jnp.float32)
    for k in range(blocks):
        top = jnp.maximum(top, jnp.abs(read(k)))
    e = jnp.ceil(STEPS * jnp.log2(top))
    write_scale(e.astype(jnp.int32).astype(jnp.int16))
    scale = LEVELS * jnp.exp2(e * (-1.0 / STEPS))
    for k in range(blocks):
        write(k, jnp.round(read(k) * scale).astype(jnp.int32).astype(jnp.int16))


def decode_scale(coded):
    return jnp.exp2(coded.astype(jnp.int32).astype(jnp.float32) * (1.0 / STEPS)) * (1.0 / LEVELS)


def encode_rows(source, i, out):
    rows, width = out.shape[1], out.shape[2] - BLK

    def write(k, value):
        out[i, :, k * BLK : (k + 1) * BLK] = value

    def write_scale(value):
        out[i, :, width:] = value

    encode(lambda k: source(k * BLK, (k + 1) * BLK), write, write_scale, width // BLK, rows)


def branch_kernel(ids, counts, hidden, tiles, keep, *refs):
    codes, (give, held, w, sems) = refs[:-4], refs[-4:]
    share = codes[0].shape[0]
    chips, rows, width = keep.shape
    blocks = width // BLK
    slots = w.shape[0]
    empty = hidden.shape[-1] // BLK
    live_count = counts[0, 0]
    parts = slots // GROUP
    tile_copies = [
        pltpu.make_async_copy(tiles.at[pl.ds(g * GROUP, GROUP)], w.at[pl.ds(g * GROUP, GROUP)], sems.at[2 + g])
        for g in range(parts)
    ]
    copies = hidden_copies(hidden, held, sems)
    for copy in copies + tile_copies:
        copy.start()
    held[:, :, :, empty * BLK :] = jnp.zeros((2, chips, rows, BLK), jnp.bfloat16)
    keep[...] = jnp.zeros_like(keep)
    give[...] = jnp.zeros_like(give)
    for copy in copies:
        copy.wait()
    for g in range(parts):
        tile_copies[g].wait()

        @pl.when(g * GROUP < live_count)
        def _(g=g):
            found = []
            for j in range(g * GROUP, (g + 1) * GROUP):
                name = ids[0, j]
                live = j < live_count
                c = jnp.where(live, name // blocks, empty)
                b = jnp.where(live, name % blocks, 0)
                left = held[:, :, :, pl.ds(pl.multiple_of(c * BLK, BLK), BLK)].reshape(2 * chips * rows, BLK)
                d = lax.dot_general(left, w[j], (((1,), (1,)), ((), ())), preferred_element_type=jnp.float32)
                found.append((b, d))
            for b, d in found:
                at = pl.ds(pl.multiple_of(b * BLK, BLK), BLK)
                keep[:, :, at] += d[: chips * rows].reshape(chips, rows, BLK)
                give[:, :, at] += d[chips * rows :].reshape(chips, rows, BLK)

    for i in range(chips):
        encode_rows(lambda lo, hi, i=i: give[i, :, lo:hi], i % share, codes[i // share])


def merge_kernel(keep, *refs):
    gots, (out, both) = refs[:-2], refs[-2:]
    chips, rows, width = keep.shape
    share = gots[0].shape[0]
    for i in range(chips):
        got, g = gots[i // share], i % share
        scale = decode_scale(got[g, :, width:])
        for k in range(width // BLK):
            at = slice(k * BLK, (k + 1) * BLK)
            both[i, :, at] = keep[i, :, at] + got[g, :, at].astype(jnp.int32).astype(jnp.float32) * scale
        encode_rows(lambda lo, hi, i=i: both[i, :, lo:hi], i, out)


def total_kernel(parts, residual, out):
    count, rows, width = parts.shape[0], out.shape[1], out.shape[2]
    scales = [decode_scale(parts[i, :, width:]) for i in range(count)]
    for k in range(width // BLK):
        at = slice(k * BLK, (k + 1) * BLK)
        value = jnp.zeros((rows, BLK), jnp.float32)
        for i in range(count):
            value += parts[i, :, at].astype(jnp.int32).astype(jnp.float32) * scales[i]
        out[0, :, at] = (residual[:, at].astype(jnp.float32) + value).astype(out.dtype)


def weight_kernel(ids, counts, a0, a1, hidden, out, held, sems):
    chips, rows = a0.shape[:2]
    blocks = a0.shape[-1] // BLK
    slots = out.shape[0]
    live_count = counts[0, 0]
    copies = hidden_copies(hidden, held, sems)
    for copy in copies:
        copy.start()
    for copy in copies:
        copy.wait()

    def some(t, _):
        for u in range(GROUP):
            j = t * GROUP + u
            name = ids[0, j]
            live = j < live_count
            c = pl.ds(pl.multiple_of(jnp.where(live, name // blocks, 0) * BLK, BLK), BLK)
            b = pl.ds(pl.multiple_of(jnp.where(live, name % blocks, 0) * BLK, BLK), BLK)
            act = jnp.concatenate([a[:, :, b].reshape(chips * rows, BLK) for a in (a0, a1)], axis=0)
            hid = held[:, :, :, c].reshape(2 * chips * rows, BLK)
            d = lax.dot_general(act, hid, (((0,), (0,)), ((), ())), preferred_element_type=jnp.float32)
            out[j] = jnp.where(live, d, 0.0).astype(out.dtype)
        return 0

    trips = (live_count + GROUP - 1) // GROUP
    lax.fori_loop(0, trips, some, 0)

    def clear(j, _):
        out[j] = jnp.zeros((BLK, BLK), out.dtype)
        return 0

    lax.fori_loop(trips * GROUP, slots, clear, 0)


SMEM = pl.BlockSpec(memory_space=pltpu.SMEM)
VMEM = pl.BlockSpec(memory_space=pltpu.VMEM)
ANY = pl.BlockSpec(memory_space=pl.ANY)
PARAMS = pltpu.CompilerParams(vmem_limit_bytes=16 << 20)


def shards(activations, hidden_grad, residual_grad, weight_tiles, tile_ids, tile_counts):
    count = lax.axis_size("tensor")
    chips = count // 2
    rows, width = activations.shape[1:]
    slots = weight_tiles.shape[2]
    hidden_width = hidden_grad.shape[2]
    swap = [(i, i ^ 1) for i in range(count)]
    same_core = [[2 * i + c for i in range(chips)] for c in range(2)]
    in_hbm = lambda x: pltpu.with_memory_space_constraint(x, pltpu.HBM)

    acts_copies = pl.pallas_call(
        spread_kernel,
        out_shape=jax.ShapeDtypeStruct((chips, rows, width), jnp.bfloat16),
        in_specs=[ANY],
        out_specs=ANY,
        scratch_shapes=[pltpu.VMEM((rows, width), jnp.bfloat16), pltpu.SemaphoreType.DMA((chips,))],
        compiler_params=PARAMS,
        name="spread",
    )(in_hbm(activations))

    tiles, hidden, acts_copies = lax.optimization_barrier((weight_tiles[0, 0], hidden_grad[0], acts_copies))
    acts = lax.all_to_all(acts_copies, "tensor", 0, 0, axis_index_groups=same_core, tiled=True)
    tiles = in_hbm(tiles)
    hidden = in_hbm(hidden.reshape(chips, 2, rows, hidden_width))
    coded = jax.ShapeDtypeStruct((chips, rows, width + BLK), jnp.int16)
    partial = pltpu.VMEM((chips, rows, width), jnp.float32)
    share = jax.ShapeDtypeStruct((chips // PIECES, rows, width + BLK), jnp.int16)
    keep, *gives = pl.pallas_call(
        branch_kernel,
        out_shape=(jax.ShapeDtypeStruct((chips, rows, width), jnp.float32),) + (share,) * PIECES,
        in_specs=[SMEM, SMEM, ANY, ANY],
        out_specs=(VMEM,) * (1 + PIECES),
        scratch_shapes=[
            partial,
            pltpu.VMEM((2, chips, rows, hidden_width + BLK), jnp.bfloat16),
            pltpu.VMEM((slots, BLK, BLK), jnp.bfloat16),
            pltpu.SemaphoreType.DMA((2 + slots // GROUP,)),
        ],
        compiler_params=PARAMS,
        cost_estimate=pl.CostEstimate(flops=1 << 10, bytes_accessed=1 << 10, transcendentals=0),
        name="branch",
    )(tile_ids[0], tile_counts, hidden, tiles)
    gots = [lax.ppermute(give, "tensor", swap) for give in gives]
    sent = pl.pallas_call(
        merge_kernel,
        out_shape=coded,
        in_specs=[VMEM] * (1 + PIECES),
        out_specs=VMEM,
        scratch_shapes=[partial],
        compiler_params=PARAMS,
        cost_estimate=pl.CostEstimate(flops=1 << 10, bytes_accessed=1 << 10, transcendentals=0),
        name="merge",
    )(keep, *gots)
    parts = lax.all_to_all(sent, "tensor", 0, 0, axis_index_groups=same_core, tiled=True)
    acts, _ = lax.optimization_barrier((acts, sent))
    acts_other = lax.ppermute(acts, "tensor", swap)
    grads = pl.pallas_call(
        weight_kernel,
        out_shape=jax.ShapeDtypeStruct((slots, BLK, BLK), jnp.bfloat16),
        in_specs=[SMEM, SMEM, VMEM, VMEM, ANY],
        out_specs=VMEM,
        scratch_shapes=[
            pltpu.VMEM((2, chips, rows, hidden_width), jnp.bfloat16),
            pltpu.SemaphoreType.DMA((2,)),
        ],
        compiler_params=PARAMS,
        cost_estimate=pl.CostEstimate(flops=1 << 10, bytes_accessed=1 << 10, transcendentals=0),
        name="weight_grads",
    )(tile_ids[0], tile_counts, acts, acts_other, hidden)
    parts, grads = lax.optimization_barrier((parts, grads))
    total = pl.pallas_call(
        total_kernel,
        out_shape=jax.ShapeDtypeStruct((1, rows, width), jnp.bfloat16),
        in_specs=[VMEM, VMEM],
        out_specs=VMEM,
        compiler_params=PARAMS,
        name="total",
    )(parts, residual_grad[0])
    pipes = lax.axis_size("pipe")
    received = lax.ppermute(total, "pipe", [(i, i - 1) for i in range(1, pipes)])
    return received, grads[None, None]


def solution(mesh):
    return jax.shard_map(
        shards,
        mesh=mesh,
        in_specs=(
            P("pipe", "tensor", None),
            P("pipe", None, "tensor"),
            P("pipe", "tensor", None),
            P("pipe", "tensor", None, None, None),
            P("pipe", "tensor", None),
            P("pipe", "tensor"),
        ),
        out_specs=(P("pipe", "tensor", None), P("pipe", "tensor", None, None, None)),
        check_vma=False,
    )
```

```python
import jax
import jax.numpy as jnp
from jax import lax
from jax.experimental import pallas as pl
from jax.experimental.pallas import tpu as pltpu
from jax.sharding import PartitionSpec as P

BLK = 128
LEVELS = 32700.0
STEPS = 128.0
FLOOR = 2.0**-100
GROUP = 16
PIECES = 2


def spread_kernel(acts, out, held, sems):
    fetch = pltpu.make_async_copy(acts.at[0], held, sems.at[0])
    fetch.start()
    fetch.wait()
    copies = [pltpu.make_async_copy(held, out.at[i], sems.at[i]) for i in range(out.shape[0])]
    for copy in copies:
        copy.start()
    for copy in copies:
        copy.wait()


def hidden_copies(hidden, held, sems):
    core = lax.axis_index("tensor") % 2
    width = hidden.shape[-1]
    return [
        pltpu.make_async_copy(hidden.at[:, which], held.at[i, :, :, pl.ds(0, width)], sems.at[i])
        for i, which in enumerate((core, 1 - core))
    ]


def encode(read, write, write_scale, blocks, rows):
    top = jnp.full((rows, BLK), FLOOR, jnp.float32)
    for k in range(blocks):
        top = jnp.maximum(top, jnp.abs(read(k)))
    e = jnp.ceil(STEPS * jnp.log2(top))
    write_scale(e.astype(jnp.int32).astype(jnp.int16))
    scale = LEVELS * jnp.exp2(e * (-1.0 / STEPS))
    for k in range(blocks):
        write(k, jnp.round(read(k) * scale).astype(jnp.int32).astype(jnp.int16))


def decode_scale(coded):
    return jnp.exp2(coded.astype(jnp.int32).astype(jnp.float32) * (1.0 / STEPS)) * (1.0 / LEVELS)


def encode_rows(source, i, out):
    rows, width = out.shape[1], out.shape[2] - BLK

    def write(k, value):
        out[i, :, k * BLK : (k + 1) * BLK] = value

    def write_scale(value):
        out[i, :, width:] = value

    encode(lambda k: source(k * BLK, (k + 1) * BLK), write, write_scale, width // BLK, rows)


def branch_kernel(ids, counts, hidden, tiles, keep, *refs):
    codes, (held, give, w, sems) = refs[:-4], refs[-4:]
    share = codes[0].shape[0]
    chips, rows, width = keep.shape
    blocks = width // BLK
    slots = w.shape[0]
    empty = hidden.shape[-1] // BLK
    live_count = counts[0, 0]
    parts = slots // GROUP
    tile_copies = [
        pltpu.make_async_copy(tiles.at[pl.ds(g * GROUP, GROUP)], w.at[pl.ds(g * GROUP, GROUP)], sems.at[2 + g])
        for g in range(parts)
    ]
    copies = hidden_copies(hidden, held, sems)
    for copy in copies + tile_copies:
        copy.start()
    held[:, :, :, empty * BLK :] = jnp.zeros((2, chips, rows, BLK), jnp.bfloat16)
    keep[...] = jnp.zeros_like(keep)
    give[...] = jnp.zeros_like(give)
    for copy in copies:
        copy.wait()
    for g in range(parts):
        tile_copies[g].wait()

        @pl.when(g * GROUP < live_count)
        def _(g=g):
            found = []
            for j in range(g * GROUP, (g + 1) * GROUP):
                name = ids[0, j]
                live = j < live_count
                c = jnp.where(live, name // blocks, empty)
                b = jnp.where(live, name % blocks, 0)
                left = held[:, :, :, pl.ds(pl.multiple_of(c * BLK, BLK), BLK)].reshape(2 * chips * rows, BLK)
                d = lax.dot_general(left, w[j], (((1,), (1,)), ((), ())), preferred_element_type=jnp.float32)
                found.append((b, d))
            for b, d in found:
                at = pl.ds(pl.multiple_of(b * BLK, BLK), BLK)
                keep[:, :, at] += d[: chips * rows].reshape(chips, rows, BLK)
                give[:, :, at] += d[chips * rows :].reshape(chips, rows, BLK)

    for i in range(chips):
        encode_rows(lambda lo, hi, i=i: give[i, :, lo:hi], i % share, codes[i // share])


def merge_kernel(keep, *refs):
    gots, (out, both) = refs[:-2], refs[-2:]
    chips, rows, width = keep.shape
    share = gots[0].shape[0]
    for i in range(chips):
        got, g = gots[i // share], i % share
        scale = decode_scale(got[g, :, width:])
        for k in range(width // BLK):
            at = slice(k * BLK, (k + 1) * BLK)
            both[i, :, at] = keep[i, :, at] + got[g, :, at].astype(jnp.int32).astype(jnp.float32) * scale
        encode_rows(lambda lo, hi, i=i: both[i, :, lo:hi], i, out)


def total_kernel(parts, residual, out):
    count, rows, width = parts.shape[0], out.shape[1], out.shape[2]
    scales = [decode_scale(parts[i, :, width:]) for i in range(count)]
    for k in range(width // BLK):
        at = slice(k * BLK, (k + 1) * BLK)
        value = jnp.zeros((rows, BLK), jnp.float32)
        for i in range(count):
            value += parts[i, :, at].astype(jnp.int32).astype(jnp.float32) * scales[i]
        out[0, :, at] = (residual[:, at].astype(jnp.float32) + value).astype(out.dtype)


def weight_kernel(ids, counts, a0, a1, held, out, made, sems):
    chips, rows = a0.shape[:2]
    blocks = a0.shape[-1] // BLK
    slots = out.shape[0]
    live_count = counts[0, 0]
    copies = []
    for g in range(slots // GROUP):
        some = pl.ds(g * GROUP, GROUP)

        @pl.when(g * GROUP < live_count)
        def _(g=g):
            for j in range(g * GROUP, (g + 1) * GROUP):
                name = ids[0, j]
                live = j < live_count
                c = pl.ds(pl.multiple_of(jnp.where(live, name // blocks, 0) * BLK, BLK), BLK)
                b = pl.ds(pl.multiple_of(jnp.where(live, name % blocks, 0) * BLK, BLK), BLK)
                act = jnp.concatenate([a[:, :, b].reshape(chips * rows, BLK) for a in (a0, a1)], axis=0)
                hid = held[:, :, :, c].reshape(2 * chips * rows, BLK)
                d = lax.dot_general(act, hid, (((0,), (0,)), ((), ())), preferred_element_type=jnp.float32)
                made[j] = jnp.where(live, d, 0.0).astype(out.dtype)

        @pl.when(g * GROUP >= live_count)
        def _(some=some):
            made[some] = jnp.zeros((GROUP, BLK, BLK), out.dtype)

        copy = pltpu.make_async_copy(made.at[some], out.at[some], sems.at[g])
        copy.start()
        copies.append(copy)
    for copy in copies:
        copy.wait()


SMEM = pl.BlockSpec(memory_space=pltpu.SMEM)
VMEM = pl.BlockSpec(memory_space=pltpu.VMEM)
ANY = pl.BlockSpec(memory_space=pl.ANY)
PARAMS = pltpu.CompilerParams(vmem_limit_bytes=16 << 20)


def shards(activations, hidden_grad, residual_grad, weight_tiles, tile_ids, tile_counts):
    count = lax.axis_size("tensor")
    chips = count // 2
    rows, width = activations.shape[1:]
    slots = weight_tiles.shape[2]
    hidden_width = hidden_grad.shape[2]
    swap = [(i, i ^ 1) for i in range(count)]
    same_core = [[2 * i + c for i in range(chips)] for c in range(2)]
    in_hbm = lambda x: pltpu.with_memory_space_constraint(x, pltpu.HBM)

    acts_copies = pl.pallas_call(
        spread_kernel,
        out_shape=jax.ShapeDtypeStruct((chips, rows, width), jnp.bfloat16),
        in_specs=[ANY],
        out_specs=ANY,
        scratch_shapes=[pltpu.VMEM((rows, width), jnp.bfloat16), pltpu.SemaphoreType.DMA((chips,))],
        compiler_params=PARAMS,
        name="spread",
    )(in_hbm(activations))

    tiles, hidden, acts_copies = lax.optimization_barrier((weight_tiles[0, 0], hidden_grad[0], acts_copies))
    acts = lax.all_to_all(acts_copies, "tensor", 0, 0, axis_index_groups=same_core, tiled=True)
    tiles = in_hbm(tiles)
    hidden = in_hbm(hidden.reshape(chips, 2, rows, hidden_width))
    coded = jax.ShapeDtypeStruct((chips, rows, width + BLK), jnp.int16)
    partial = pltpu.VMEM((chips, rows, width), jnp.float32)
    share = jax.ShapeDtypeStruct((chips // PIECES, rows, width + BLK), jnp.int16)
    held = jax.ShapeDtypeStruct((2, chips, rows, hidden_width + BLK), jnp.bfloat16)
    keep, *gives, held = pl.pallas_call(
        branch_kernel,
        out_shape=(jax.ShapeDtypeStruct((chips, rows, width), jnp.float32),) + (share,) * PIECES + (held,),
        in_specs=[SMEM, SMEM, ANY, ANY],
        out_specs=(VMEM,) * (2 + PIECES),
        scratch_shapes=[
            partial,
            pltpu.VMEM((slots, BLK, BLK), jnp.bfloat16),
            pltpu.SemaphoreType.DMA((2 + slots // GROUP,)),
        ],
        compiler_params=PARAMS,
        cost_estimate=pl.CostEstimate(flops=1 << 10, bytes_accessed=1 << 10, transcendentals=0),
        name="branch",
    )(tile_ids[0], tile_counts, hidden, tiles)
    gots = [lax.ppermute(give, "tensor", swap) for give in gives]
    sent = pl.pallas_call(
        merge_kernel,
        out_shape=coded,
        in_specs=[VMEM] * (1 + PIECES),
        out_specs=VMEM,
        scratch_shapes=[partial],
        compiler_params=PARAMS,
        cost_estimate=pl.CostEstimate(flops=1 << 10, bytes_accessed=1 << 10, transcendentals=0),
        name="merge",
    )(keep, *gots)
    acts, sent = lax.optimization_barrier((acts, sent))
    acts_other = lax.ppermute(acts, "tensor", swap)
    residual = residual_grad[0]
    pipes = lax.axis_size("pipe")
    late = pipes // 2 - 1
    is_late = lax.axis_index("pipe") == late

    def reduced(sent, residual):
        parts = lax.all_to_all(sent, "tensor", 0, 0, axis_index_groups=same_core, tiled=True)
        return pl.pallas_call(
            total_kernel,
            out_shape=jax.ShapeDtypeStruct((1, rows, width), jnp.bfloat16),
            in_specs=[VMEM, VMEM],
            out_specs=VMEM,
            compiler_params=PARAMS,
            name="total",
        )(parts, residual)

    early = lax.cond(
        is_late,
        lambda sent, residual: jnp.zeros((1, rows, width), jnp.bfloat16),
        reduced,
        sent,
        residual,
    )
    most = lax.ppermute(early, "pipe", [(i, i - 1) for i in range(1, pipes) if i != late])
    sent, _ = lax.optimization_barrier((sent, early))
    behind = lax.cond(
        is_late,
        reduced,
        lambda sent, residual: jnp.zeros((1, rows, width), jnp.bfloat16),
        sent,
        residual,
    )
    rest = lax.ppermute(behind, "pipe", [(late, late - 1)])
    grads = pl.pallas_call(
        weight_kernel,
        out_shape=jax.ShapeDtypeStruct((slots, BLK, BLK), jnp.bfloat16),
        in_specs=[SMEM, SMEM, VMEM, VMEM, VMEM],
        out_specs=ANY,
        scratch_shapes=[
            pltpu.VMEM((slots, BLK, BLK), jnp.bfloat16),
            pltpu.SemaphoreType.DMA((slots // GROUP,)),
        ],
        compiler_params=PARAMS,
        cost_estimate=pl.CostEstimate(flops=4 << 30, bytes_accessed=6 << 20, transcendentals=0),
        name="weight_grads",
    )(tile_ids[0], tile_counts, acts, lax.optimization_barrier((acts_other, behind))[0], held)
    rest, most, grads = lax.optimization_barrier((rest, most, grads))
    received = jnp.where(lax.axis_index("pipe") == late - 1, rest, most)
    return received, grads[None, None]


def solution(mesh):
    return jax.shard_map(
        shards,
        mesh=mesh,
        in_specs=(
            P("pipe", "tensor", None),
            P("pipe", None, "tensor"),
            P("pipe", "tensor", None),
            P("pipe", "tensor", None, None, None),
            P("pipe", "tensor", None),
            P("pipe", "tensor"),
        ),
        out_specs=(P("pipe", "tensor", None), P("pipe", "tensor", None, None, None)),
        check_vma=False,
    )
```

```python
import jax
import jax.numpy as jnp
from jax import lax
from jax.experimental import pallas as pl
from jax.experimental.pallas import tpu as pltpu
from jax.sharding import PartitionSpec as P

BLK = 128
LEVELS = 32700.0
STEPS = 128.0
FLOOR = 2.0**-100
GROUP = 16
PIECES = 2


def spread_kernel(acts, out, held, sems):
    fetch = pltpu.make_async_copy(acts.at[0], held, sems.at[0])
    fetch.start()
    fetch.wait()
    copies = [pltpu.make_async_copy(held, out.at[i], sems.at[i]) for i in range(out.shape[0])]
    for copy in copies:
        copy.start()
    for copy in copies:
        copy.wait()


def hidden_copies(hidden, held, sems):
    core = lax.axis_index("tensor") % 2
    width = hidden.shape[-1]
    return [
        pltpu.make_async_copy(hidden.at[:, which], held.at[i, :, :, pl.ds(0, width)], sems.at[i])
        for i, which in enumerate((core, 1 - core))
    ]


def encode(read, write, write_scale, blocks, rows):
    top = jnp.full((rows, BLK), FLOOR, jnp.float32)
    for k in range(blocks):
        top = jnp.maximum(top, jnp.abs(read(k)))
    e = jnp.ceil(STEPS * jnp.log2(top))
    write_scale(e.astype(jnp.int32).astype(jnp.int16))
    scale = LEVELS * jnp.exp2(e * (-1.0 / STEPS))
    for k in range(blocks):
        write(k, jnp.round(read(k) * scale).astype(jnp.int32).astype(jnp.int16))


def decode_scale(coded):
    return jnp.exp2(coded.astype(jnp.int32).astype(jnp.float32) * (1.0 / STEPS)) * (1.0 / LEVELS)


def encode_rows(source, i, out):
    rows, width = out.shape[1], out.shape[2] - BLK

    def write(k, value):
        out[i, :, k * BLK : (k + 1) * BLK] = value

    def write_scale(value):
        out[i, :, width:] = value

    encode(lambda k: source(k * BLK, (k + 1) * BLK), write, write_scale, width // BLK, rows)


def branch_kernel(ids, counts, hidden, tiles, keep, *refs):
    codes, (turned, held, give, w, sems) = refs[:-5], refs[-5:]
    share = codes[0].shape[0]
    chips, rows, width = keep.shape
    blocks = width // BLK
    slots = w.shape[0]
    empty = hidden.shape[-1] // BLK
    live_count = counts[0, 0]
    parts = slots // GROUP
    tile_copies = [
        pltpu.make_async_copy(tiles.at[pl.ds(g * GROUP, GROUP)], w.at[pl.ds(g * GROUP, GROUP)], sems.at[2 + g])
        for g in range(parts)
    ]
    copies = hidden_copies(hidden, held, sems)
    for copy in copies + tile_copies:
        copy.start()
    held[:, :, :, empty * BLK :] = jnp.zeros((2, chips, rows, BLK), jnp.bfloat16)
    keep[...] = jnp.zeros_like(keep)
    give[...] = jnp.zeros_like(give)
    for copy in copies:
        copy.wait()
    for c in range(empty):
        at = slice(c * BLK, (c + 1) * BLK)
        turned[at, :] = held[:, :, :, at].reshape(2 * chips * rows, BLK).T
    for g in range(parts):
        tile_copies[g].wait()

        @pl.when(g * GROUP < live_count)
        def _(g=g):
            found = []
            for j in range(g * GROUP, (g + 1) * GROUP):
                name = ids[0, j]
                live = j < live_count
                c = jnp.where(live, name // blocks, empty)
                b = jnp.where(live, name % blocks, 0)
                left = held[:, :, :, pl.ds(pl.multiple_of(c * BLK, BLK), BLK)].reshape(2 * chips * rows, BLK)
                d = lax.dot_general(left, w[j], (((1,), (1,)), ((), ())), preferred_element_type=jnp.float32)
                found.append((b, d))
            for b, d in found:
                at = pl.ds(pl.multiple_of(b * BLK, BLK), BLK)
                keep[:, :, at] += d[: chips * rows].reshape(chips, rows, BLK)
                give[:, :, at] += d[chips * rows :].reshape(chips, rows, BLK)

    for i in range(chips):
        encode_rows(lambda lo, hi, i=i: give[i, :, lo:hi], i % share, codes[i // share])


def merge_kernel(keep, *refs):
    gots, (out, both, coded, sems) = refs[:-4], refs[-4:]
    chips, rows, width = keep.shape
    share = gots[0].shape[0]
    copies = []
    for i in range(chips):
        got, g = gots[i // share], i % share
        scale = decode_scale(got[g, :, width:])
        for k in range(width // BLK):
            at = slice(k * BLK, (k + 1) * BLK)
            both[i, :, at] = keep[i, :, at] + got[g, :, at].astype(jnp.int32).astype(jnp.float32) * scale
        encode_rows(lambda lo, hi, i=i: both[i, :, lo:hi], i, coded)
        copies.append(pltpu.make_async_copy(coded.at[i], out.at[i], sems.at[i]))
        copies[-1].start()
    for copy in copies:
        copy.wait()


def total_kernel(parts, residual, out):
    count, rows, width = parts.shape[0], out.shape[1], out.shape[2]
    scales = [decode_scale(parts[i, :, width:]) for i in range(count)]
    for k in range(width // BLK):
        at = slice(k * BLK, (k + 1) * BLK)
        value = jnp.zeros((rows, BLK), jnp.float32)
        for i in range(count):
            value += parts[i, :, at].astype(jnp.int32).astype(jnp.float32) * scales[i]
        out[0, :, at] = (residual[:, at].astype(jnp.float32) + value).astype(out.dtype)


def weight_kernel(ids, counts, a0, a1, turned, out, made, sems):
    chips, rows = a0.shape[:2]
    blocks = a0.shape[-1] // BLK
    slots = out.shape[0]
    live_count = counts[0, 0]
    copies = []
    for g in range(slots // GROUP):
        some = pl.ds(g * GROUP, GROUP)

        @pl.when(g * GROUP < live_count)
        def _(g=g):
            for j in range(g * GROUP, (g + 1) * GROUP):
                name = ids[0, j]
                live = j < live_count
                c = pl.ds(pl.multiple_of(jnp.where(live, name // blocks, 0) * BLK, BLK), BLK)
                b = pl.ds(pl.multiple_of(jnp.where(live, name % blocks, 0) * BLK, BLK), BLK)
                act = jnp.concatenate([a[:, :, b].reshape(chips * rows, BLK) for a in (a0, a1)], axis=0)
                d = jnp.dot(turned[c, :], act, preferred_element_type=jnp.float32)
                made[j] = jnp.where(live, d, 0.0).astype(out.dtype).T

        @pl.when(g * GROUP >= live_count)
        def _(some=some):
            made[some] = jnp.zeros((GROUP, BLK, BLK), out.dtype)

        copy = pltpu.make_async_copy(made.at[some], out.at[some], sems.at[g])
        copy.start()
        copies.append(copy)
    for copy in copies:
        copy.wait()


SMEM = pl.BlockSpec(memory_space=pltpu.SMEM)
VMEM = pl.BlockSpec(memory_space=pltpu.VMEM)
ANY = pl.BlockSpec(memory_space=pl.ANY)
PARAMS = pltpu.CompilerParams(vmem_limit_bytes=16 << 20)


def shards(activations, hidden_grad, residual_grad, weight_tiles, tile_ids, tile_counts):
    count = lax.axis_size("tensor")
    chips = count // 2
    rows, width = activations.shape[1:]
    slots = weight_tiles.shape[2]
    hidden_width = hidden_grad.shape[2]
    swap = [(i, i ^ 1) for i in range(count)]
    same_core = [[2 * i + c for i in range(chips)] for c in range(2)]
    in_hbm = lambda x: pltpu.with_memory_space_constraint(x, pltpu.HBM)

    acts_copies = pl.pallas_call(
        spread_kernel,
        out_shape=jax.ShapeDtypeStruct((chips, rows, width), jnp.bfloat16),
        in_specs=[ANY],
        out_specs=ANY,
        scratch_shapes=[pltpu.VMEM((rows, width), jnp.bfloat16), pltpu.SemaphoreType.DMA((chips,))],
        compiler_params=PARAMS,
        name="spread",
    )(in_hbm(activations))

    tiles, hidden, acts_copies = lax.optimization_barrier((weight_tiles[0, 0], hidden_grad[0], acts_copies))
    acts = lax.all_to_all(acts_copies, "tensor", 0, 0, axis_index_groups=same_core, tiled=True)
    tiles = in_hbm(tiles)
    hidden = in_hbm(hidden.reshape(chips, 2, rows, hidden_width))
    coded = jax.ShapeDtypeStruct((chips, rows, width + BLK), jnp.int16)
    partial = pltpu.VMEM((chips, rows, width), jnp.float32)
    share = jax.ShapeDtypeStruct((chips // PIECES, rows, width + BLK), jnp.int16)
    turned = jax.ShapeDtypeStruct((hidden_width, 2 * chips * rows), jnp.bfloat16)
    keep, *gives, turned = pl.pallas_call(
        branch_kernel,
        out_shape=(jax.ShapeDtypeStruct((chips, rows, width), jnp.float32),) + (share,) * PIECES + (turned,),
        in_specs=[SMEM, SMEM, ANY, ANY],
        out_specs=(VMEM,) * (2 + PIECES),
        scratch_shapes=[
            pltpu.VMEM((2, chips, rows, hidden_width + BLK), jnp.bfloat16),
            partial,
            pltpu.VMEM((slots, BLK, BLK), jnp.bfloat16),
            pltpu.SemaphoreType.DMA((2 + slots // GROUP,)),
        ],
        compiler_params=PARAMS,
        cost_estimate=pl.CostEstimate(flops=1 << 10, bytes_accessed=1 << 10, transcendentals=0),
        name="branch",
    )(tile_ids[0], tile_counts, hidden, tiles)
    gots = [lax.ppermute(give, "tensor", swap) for give in gives]
    sent = pl.pallas_call(
        merge_kernel,
        out_shape=coded,
        in_specs=[VMEM] * (1 + PIECES),
        out_specs=ANY,
        scratch_shapes=[partial, pltpu.VMEM(coded.shape, jnp.int16), pltpu.SemaphoreType.DMA((chips,))],
        compiler_params=PARAMS,
        cost_estimate=pl.CostEstimate(flops=1 << 10, bytes_accessed=1 << 10, transcendentals=0),
        name="merge",
    )(keep, *gots)
    acts, sent = lax.optimization_barrier((acts, sent))
    acts_other = lax.ppermute(acts, "tensor", swap)
    residual = residual_grad[0]
    pipes = lax.axis_size("pipe")
    late = pipes // 2 - 1
    is_late = lax.axis_index("pipe") == late

    def reduced(sent, residual):
        parts = lax.all_to_all(sent, "tensor", 0, 0, axis_index_groups=same_core, tiled=True)
        return pl.pallas_call(
            total_kernel,
            out_shape=jax.ShapeDtypeStruct((1, rows, width), jnp.bfloat16),
            in_specs=[VMEM, VMEM],
            out_specs=VMEM,
            compiler_params=PARAMS,
            name="total",
        )(parts, residual)

    early = lax.cond(
        is_late,
        lambda sent, residual: jnp.zeros((1, rows, width), jnp.bfloat16),
        reduced,
        sent,
        residual,
    )
    over = lax.ppermute(early, "pipe", [(late + 1, late)])
    sent, _ = lax.optimization_barrier((sent, early))
    behind = lax.cond(
        is_late,
        reduced,
        lambda sent, residual: jnp.zeros((1, rows, width), jnp.bfloat16),
        sent,
        residual,
    )
    behind, early = lax.optimization_barrier((behind, early))
    most = lax.ppermute(early, "pipe", [(i, i - 1) for i in range(1, pipes) if i not in (late, late + 1)])
    rest = lax.ppermute(behind, "pipe", [(late, late - 1)])
    grads = pl.pallas_call(
        weight_kernel,
        out_shape=jax.ShapeDtypeStruct((slots, BLK, BLK), jnp.bfloat16),
        in_specs=[SMEM, SMEM, VMEM, VMEM, VMEM],
        out_specs=ANY,
        scratch_shapes=[
            pltpu.VMEM((slots, BLK, BLK), jnp.bfloat16),
            pltpu.SemaphoreType.DMA((slots // GROUP,)),
        ],
        compiler_params=PARAMS,
        cost_estimate=pl.CostEstimate(flops=4 << 30, bytes_accessed=6 << 20, transcendentals=0),
        name="weight_grads",
    )(tile_ids[0], tile_counts, acts, lax.optimization_barrier((acts_other, behind))[0], turned)
    rest, most, grads = lax.optimization_barrier((rest, most, grads))
    place = lax.axis_index("pipe")
    received = jnp.where(place == late, over, jnp.where(place == late - 1, rest, most))
    return received, grads[None, None]


def solution(mesh):
    return jax.shard_map(
        shards,
        mesh=mesh,
        in_specs=(
            P("pipe", "tensor", None),
            P("pipe", None, "tensor"),
            P("pipe", "tensor", None),
            P("pipe", "tensor", None, None, None),
            P("pipe", "tensor", None),
            P("pipe", "tensor"),
        ),
        out_specs=(P("pipe", "tensor", None), P("pipe", "tensor", None, None, None)),
        check_vma=False,
    )
```

```python
import jax
import jax.numpy as jnp
from jax import lax
from jax.experimental import pallas as pl
from jax.experimental.pallas import tpu as pltpu
from jax.sharding import PartitionSpec as P

BLK = 128
LEVELS = 32700.0
STEPS = 128.0
FLOOR = 2.0**-100
GROUP = 16
PIECES = 2


def spread_kernel(acts, out, held, sems):
    fetch = pltpu.make_async_copy(acts.at[0], held, sems.at[0])
    fetch.start()
    fetch.wait()
    copies = [pltpu.make_async_copy(held, out.at[i], sems.at[i]) for i in range(out.shape[0])]
    for copy in copies:
        copy.start()
    for copy in copies:
        copy.wait()


def hidden_copies(hidden, held, sems):
    core = lax.axis_index("tensor") % 2
    width = hidden.shape[-1]
    return [
        pltpu.make_async_copy(hidden.at[:, which], held.at[i, :, :, pl.ds(0, width)], sems.at[i])
        for i, which in enumerate((core, 1 - core))
    ]


def encode(read, write, write_scale, blocks, rows):
    top = jnp.full((rows, BLK), FLOOR, jnp.float32)
    for k in range(blocks):
        top = jnp.maximum(top, jnp.abs(read(k)))
    e = jnp.ceil(STEPS * jnp.log2(top))
    write_scale(e.astype(jnp.int32).astype(jnp.int16))
    scale = LEVELS * jnp.exp2(e * (-1.0 / STEPS))
    for k in range(blocks):
        write(k, jnp.round(read(k) * scale).astype(jnp.int32).astype(jnp.int16))


def decode_scale(coded):
    return jnp.exp2(coded.astype(jnp.int32).astype(jnp.float32) * (1.0 / STEPS)) * (1.0 / LEVELS)


def encode_rows(source, i, out):
    rows, width = out.shape[1], out.shape[2] - BLK

    def write(k, value):
        out[i, :, k * BLK : (k + 1) * BLK] = value

    def write_scale(value):
        out[i, :, width:] = value

    encode(lambda k: source(k * BLK, (k + 1) * BLK), write, write_scale, width // BLK, rows)


def branch_kernel(ids, counts, hidden, tiles, keep, *refs):
    codes, (turned, held, give, w, sems) = refs[:-5], refs[-5:]
    share = codes[0].shape[0]
    chips, rows, width = keep.shape
    blocks = width // BLK
    slots = w.shape[0]
    empty = hidden.shape[-1] // BLK
    live_count = counts[0, 0]
    parts = slots // GROUP
    tile_copies = [
        pltpu.make_async_copy(tiles.at[pl.ds(g * GROUP, GROUP)], w.at[pl.ds(g * GROUP, GROUP)], sems.at[2 + g])
        for g in range(parts)
    ]
    copies = hidden_copies(hidden, held, sems)
    for copy in copies + tile_copies:
        copy.start()
    held[:, :, :, empty * BLK :] = jnp.zeros((2, chips, rows, BLK), jnp.bfloat16)
    keep[...] = jnp.zeros_like(keep)
    give[...] = jnp.zeros_like(give)
    for copy in copies:
        copy.wait()
    for c in range(empty):
        at = slice(c * BLK, (c + 1) * BLK)
        turned[at, :] = held[:, :, :, at].reshape(2 * chips * rows, BLK).T
    for g in range(parts):
        tile_copies[g].wait()

        @pl.when(g * GROUP < live_count)
        def _(g=g):
            found = []
            for j in range(g * GROUP, (g + 1) * GROUP):
                name = ids[0, j]
                live = j < live_count
                c = jnp.where(live, name // blocks, empty)
                b = jnp.where(live, name % blocks, 0)
                left = held[:, :, :, pl.ds(pl.multiple_of(c * BLK, BLK), BLK)].reshape(2 * chips * rows, BLK)
                d = lax.dot_general(left, w[j], (((1,), (1,)), ((), ())), preferred_element_type=jnp.float32)
                found.append((b, d))
            for b, d in found:
                at = pl.ds(pl.multiple_of(b * BLK, BLK), BLK)
                keep[:, :, at] += d[: chips * rows].reshape(chips, rows, BLK)
                give[:, :, at] += d[chips * rows :].reshape(chips, rows, BLK)

    for i in range(chips):
        encode_rows(lambda lo, hi, i=i: give[i, :, lo:hi], i % share, codes[i // share])


def merge_kernel(keep, *refs):
    gots, (out, both, coded, sems) = refs[:-4], refs[-4:]
    chips, rows, width = keep.shape
    share = gots[0].shape[0]
    copies = []
    for i in range(chips):
        got, g = gots[i // share], i % share
        scale = decode_scale(got[g, :, width:])
        for k in range(width // BLK):
            at = slice(k * BLK, (k + 1) * BLK)
            both[i, :, at] = keep[i, :, at] + got[g, :, at].astype(jnp.int32).astype(jnp.float32) * scale
        encode_rows(lambda lo, hi, i=i: both[i, :, lo:hi], i, coded)
        copies.append(pltpu.make_async_copy(coded.at[i], out.at[i], sems.at[i]))
        copies[-1].start()
    for copy in copies:
        copy.wait()


def total_kernel(parts, residual, out, again):
    count, rows, width = parts.shape[0], out.shape[1], out.shape[2]
    scales = [decode_scale(parts[i, :, width:]) for i in range(count)]
    for k in range(width // BLK):
        at = slice(k * BLK, (k + 1) * BLK)
        value = jnp.zeros((rows, BLK), jnp.float32)
        for i in range(count):
            value += parts[i, :, at].astype(jnp.int32).astype(jnp.float32) * scales[i]
        out[0, :, at] = again[0, :, at] = (residual[:, at].astype(jnp.float32) + value).astype(out.dtype)


def weight_kernel(ids, counts, a0, a1, turned, out, made, sems):
    chips, rows = a0.shape[:2]
    blocks = a0.shape[-1] // BLK
    slots = out.shape[0]
    live_count = counts[0, 0]
    copies = []
    for g in range(slots // GROUP):
        some = pl.ds(g * GROUP, GROUP)

        @pl.when(g * GROUP < live_count)
        def _(g=g):
            for j in range(g * GROUP, (g + 1) * GROUP):
                name = ids[0, j]
                live = j < live_count
                c = pl.ds(pl.multiple_of(jnp.where(live, name // blocks, 0) * BLK, BLK), BLK)
                b = pl.ds(pl.multiple_of(jnp.where(live, name % blocks, 0) * BLK, BLK), BLK)
                act = jnp.concatenate([a[:, :, b].reshape(chips * rows, BLK) for a in (a0, a1)], axis=0)
                d = jnp.dot(turned[c, :], act, preferred_element_type=jnp.float32)
                made[j] = jnp.where(live, d, 0.0).astype(out.dtype).T

        @pl.when(g * GROUP >= live_count)
        def _(some=some):
            made[some] = jnp.zeros((GROUP, BLK, BLK), out.dtype)

        copy = pltpu.make_async_copy(made.at[some], out.at[some], sems.at[g])
        copy.start()
        copies.append(copy)
    for copy in copies:
        copy.wait()


SMEM = pl.BlockSpec(memory_space=pltpu.SMEM)
VMEM = pl.BlockSpec(memory_space=pltpu.VMEM)
ANY = pl.BlockSpec(memory_space=pl.ANY)
PARAMS = pltpu.CompilerParams(vmem_limit_bytes=16 << 20)


def shards(activations, hidden_grad, residual_grad, weight_tiles, tile_ids, tile_counts):
    count = lax.axis_size("tensor")
    chips = count // 2
    rows, width = activations.shape[1:]
    slots = weight_tiles.shape[2]
    hidden_width = hidden_grad.shape[2]
    swap = [(i, i ^ 1) for i in range(count)]
    same_core = [[2 * i + c for i in range(chips)] for c in range(2)]
    in_hbm = lambda x: pltpu.with_memory_space_constraint(x, pltpu.HBM)

    acts_copies = pl.pallas_call(
        spread_kernel,
        out_shape=jax.ShapeDtypeStruct((chips, rows, width), jnp.bfloat16),
        in_specs=[ANY],
        out_specs=ANY,
        scratch_shapes=[pltpu.VMEM((rows, width), jnp.bfloat16), pltpu.SemaphoreType.DMA((chips,))],
        compiler_params=PARAMS,
        name="spread",
    )(in_hbm(activations))

    tiles, hidden, acts_copies = lax.optimization_barrier((weight_tiles[0, 0], hidden_grad[0], acts_copies))
    acts = lax.all_to_all(acts_copies, "tensor", 0, 0, axis_index_groups=same_core, tiled=True)
    tiles = in_hbm(tiles)
    hidden = in_hbm(hidden.reshape(chips, 2, rows, hidden_width))
    coded = jax.ShapeDtypeStruct((chips, rows, width + BLK), jnp.int16)
    partial = pltpu.VMEM((chips, rows, width), jnp.float32)
    share = jax.ShapeDtypeStruct((chips // PIECES, rows, width + BLK), jnp.int16)
    turned = jax.ShapeDtypeStruct((hidden_width, 2 * chips * rows), jnp.bfloat16)
    keep, *gives, turned = pl.pallas_call(
        branch_kernel,
        out_shape=(jax.ShapeDtypeStruct((chips, rows, width), jnp.float32),) + (share,) * PIECES + (turned,),
        in_specs=[SMEM, SMEM, ANY, ANY],
        out_specs=(VMEM,) * (2 + PIECES),
        scratch_shapes=[
            pltpu.VMEM((2, chips, rows, hidden_width + BLK), jnp.bfloat16),
            partial,
            pltpu.VMEM((slots, BLK, BLK), jnp.bfloat16),
            pltpu.SemaphoreType.DMA((2 + slots // GROUP,)),
        ],
        compiler_params=PARAMS,
        cost_estimate=pl.CostEstimate(flops=1 << 10, bytes_accessed=1 << 10, transcendentals=0),
        name="branch",
    )(tile_ids[0], tile_counts, hidden, tiles)
    gots = [lax.ppermute(give, "tensor", swap) for give in gives]
    sent = pl.pallas_call(
        merge_kernel,
        out_shape=coded,
        in_specs=[VMEM] * (1 + PIECES),
        out_specs=ANY,
        scratch_shapes=[partial, pltpu.VMEM(coded.shape, jnp.int16), pltpu.SemaphoreType.DMA((chips,))],
        compiler_params=PARAMS,
        cost_estimate=pl.CostEstimate(flops=1 << 10, bytes_accessed=1 << 10, transcendentals=0),
        name="merge",
    )(keep, *gots)
    acts, sent = lax.optimization_barrier((acts, sent))
    acts_other = lax.ppermute(acts, "tensor", swap)
    residual = residual_grad[0]
    pipes = lax.axis_size("pipe")
    late = pipes // 2 - 1
    is_late = lax.axis_index("pipe") == late

    def reduced(sent, residual):
        parts = lax.all_to_all(sent, "tensor", 0, 0, axis_index_groups=same_core, tiled=True)
        return pl.pallas_call(
            total_kernel,
            out_shape=(jax.ShapeDtypeStruct((1, rows, width), jnp.bfloat16),) * 2,
            in_specs=[VMEM, VMEM],
            out_specs=(VMEM, VMEM),
            compiler_params=PARAMS,
            name="total",
        )(parts, residual)

    def nothing(sent, residual):
        return (jnp.zeros((1, rows, width), jnp.bfloat16),) * 2

    crossing, early = lax.cond(is_late, nothing, reduced, sent, residual)
    over = lax.ppermute(crossing, "pipe", [(late + 1, late)])
    sent, early = lax.optimization_barrier((sent, early))
    total = lax.cond(
        is_late,
        lambda early, sent, residual: reduced(sent, residual)[0],
        lambda early, sent, residual: early,
        early,
        sent,
        residual,
    )
    total, over = lax.optimization_barrier((total, over))
    most = lax.ppermute(total, "pipe", [(i, i - 1) for i in range(1, pipes) if i != late + 1])
    grads = pl.pallas_call(
        weight_kernel,
        out_shape=jax.ShapeDtypeStruct((slots, BLK, BLK), jnp.bfloat16),
        in_specs=[SMEM, SMEM, VMEM, VMEM, VMEM],
        out_specs=ANY,
        scratch_shapes=[
            pltpu.VMEM((slots, BLK, BLK), jnp.bfloat16),
            pltpu.SemaphoreType.DMA((slots // GROUP,)),
        ],
        compiler_params=PARAMS,
        cost_estimate=pl.CostEstimate(flops=4 << 30, bytes_accessed=6 << 20, transcendentals=0),
        name="weight_grads",
    )(tile_ids[0], tile_counts, acts, lax.optimization_barrier((acts_other, total))[0], turned)
    most, grads = lax.optimization_barrier((most, grads))
    received = jnp.where(is_late, over, most)
    return received, grads[None, None]


def solution(mesh):
    return jax.shard_map(
        shards,
        mesh=mesh,
        in_specs=(
            P("pipe", "tensor", None),
            P("pipe", None, "tensor"),
            P("pipe", "tensor", None),
            P("pipe", "tensor", None, None, None),
            P("pipe", "tensor", None),
            P("pipe", "tensor"),
        ),
        out_specs=(P("pipe", "tensor", None), P("pipe", "tensor", None, None, None)),
        check_vma=False,
    )
```
